32 devices in a mesh: dp: 2 (over x), ctx: 4 (over y, core), exp: 4 (over z).
Axes of the slice: x: 2, y: 2, z: 4, core: 2. Of those that a mesh axis runs over, the one named last changes fastest.
Arguments:
- block_input: bfloat16 [8, 1024, 1024], P(('dp', 'exp'), 'ctx'), may hold values from -6 to 6
- positions: int32 [8, 1024], P(('dp', 'exp')), may hold values from 0 to 1023, as said below
- norm_gain: bfloat16 [1024], replicated, may hold values from 0.5 to 1.5
- query_weight: bfloat16 [1024, 1024], replicated, may hold values from -0.1875 to 0.1875
- key_weight: bfloat16 [1024, 512], replicated, may hold values from -0.1875 to 0.1875
- value_weight: bfloat16 [1024, 512], replicated, may hold values from -0.1875 to 0.1875
- output_weight: bfloat16 [1024, 1024], replicated, may hold values from -3 to 3
- mixer_gain: bfloat16 [1024], replicated, may hold values from 0.5 to 1.5
- router_weight: bfloat16 [1024, 32], replicated, may hold values from -0.09375 to 0.09375
- expert_gate: bfloat16 [32, 1024, 512], P(('ctx', 'exp')), may hold values from -0.1875 to 0.1875
- expert_up: bfloat16 [32, 1024, 512], P(('ctx', 'exp')), may hold values from -0.1875 to 0.1875
- expert_down: bfloat16 [32, 512, 1024], P(('ctx', 'exp')), may hold values from -1 to 1
- routes: int32 [8, 1024, 8], P(('dp', 'exp'), 'ctx'), may hold values from 0 to 31, all different within a row; in each aligned block of 256 rows (0 to 255, 256 to 511, ..., all dimensions but the last counted through in order) at most 128 rows name the same one
- cotangent: bfloat16 [8, 1024, 1024], P(('dp', 'exp'), 'ctx'), may hold values from -6 to 6
Outputs:
- out: bfloat16 [8, 1024, 1024], P(('dp', 'exp'), 'ctx')
- input_grad: bfloat16 [8, 1024, 1024], P(('dp', 'exp'), 'ctx')
- norm_gain_grad: float32 [1024], replicated
- query_grad: float32 [1024, 1024], replicated
- key_grad: float32 [1024, 512], replicated
- value_grad: float32 [1024, 512], replicated
- output_grad: float32 [1024, 1024], replicated
- mixer_gain_grad: float32 [1024], replicated
- router_grad: float32 [1024, 32], replicated
- gate_grad: float32 [32, 1024, 512], P(('ctx', 'exp'), 'dp')
- up_grad: float32 [32, 1024, 512], P(('ctx', 'exp'), 'dp')
- down_grad: float32 [32, 512, 1024], P(('ctx', 'exp'), 'dp')
The draws below stay inside these ranges and needn't reach their ends.
Inputs may be any that keep to these rules, and one draw needn't show every extreme that they name: Within each sequence the positions are a permutation of 0 to 1023, made of runs of 128 consecutive rising positions, each run starting at a multiple of 128. `routes`: among the 256 tokens of one sequence block on one index of ctx, no expert is named more than 128 times.
All inputs are finite; a program needn't handle non-finite values.
Results may differ from the reference program's by a relative error of at most 0.018.
Values may be sent and summed in bfloat16 or wider, within the bound.
A program may use at most 192 MiB of HBM per device.

```python
import math
import jax
import jax.numpy as jnp
import numpy as np
from jax import lax

D = 1024
HEADS = 16
KV_HEADS = 8
HD = 64
FF = 512
TOP = 8
STRETCH = 256
EXPERTS = 32
SEQS = 8
LENGTH = 1024
CAP = 128
N_CTX = 4


def draw_positions(key, part):
    half = STRETCH // 2
    pieces = 2 * N_CTX
    keys = jax.random.split(jax.random.fold_in(key, 7), SEQS)
    orders = jax.vmap(lambda k: jax.random.permutation(k, pieces))(keys).astype(jnp.int32)
    within = jnp.arange(half, dtype=jnp.int32)
    places = orders[:, :, None] * half + within[None, None, :]
    return places.reshape(SEQS, LENGTH).astype(jnp.int32)


def steps_of(rng, extent, cuts, low, high):
    level = 1.0
    for position, blocks in cuts:
        steps = jax.random.uniform(jax.random.fold_in(jax.random.fold_in(rng, 6), position), (blocks,), jnp.float32, low / len(cuts), high / len(cuts))
        level = level * jnp.repeat(jnp.exp(steps), extent[position] // blocks).reshape((-1,) + (1,) * (len(extent) - 1 - position))
    return level


def deal_out(rng, own, number, rows, amount, top, limit, skew):
    order = jax.random.permutation(rng, amount)
    packed, usual = load_shares(amount, rows * top, limit, skew, True), load_shares(amount, rows * top, limit, skew, False)
    places = jnp.arange(amount)

    def named(tallies, offset_by):
        used = int((tallies > 0).sum())
        fixed = max(1, used // 4)
        passed = fixed + (places - fixed + offset_by * (used - fixed)) % max(1, amount - fixed)
        return jnp.zeros((amount,), jnp.int32).at[order[jnp.where(places < fixed, places, passed)]].set(jnp.asarray(tallies, jnp.int32))

    tallies = jnp.where(number % 4 == 0, named(packed, number // 4), named(usual, number - number // 4 - 1))
    mixed = jax.random.permutation(jax.random.fold_in(own, 3), amount)
    giver, receiver = mixed[0:amount // 2 * 2:2], mixed[1:amount // 2 * 2:2]
    room = jnp.minimum(tallies[giver] - 1, limit - tallies[receiver]) // 2
    room = jnp.where((giver == order[0]) | (receiver == order[0]) | (tallies[receiver] == 0), 0, jnp.maximum(room, 0))
    passed = jax.random.randint(jax.random.fold_in(own, 4), (amount // 2,), 0, 1 << 20) % (room + 1)
    tallies = tallies.at[giver].add(-passed).at[receiver].add(passed)
    members = jnp.searchsorted(jnp.cumsum(tallies), jnp.arange(rows * top), side="right").astype(jnp.int32)
    table = members.reshape(top, rows).T
    table = table[jax.random.permutation(jax.random.fold_in(own, 1), rows)]
    offset_by = jax.random.randint(jax.random.fold_in(own, 2), (rows, 1), 0, top)
    return jnp.take_along_axis(table, (jnp.arange(top)[None, :] + offset_by) % top, axis=1)


def load_shares(amount, total, most, slope, full):
    loads = [(1 << 20) // math.isqrt(standing ** slope) + 1 for standing in range(1, amount + 1)]
    largest = most if full else min(most, max(-(-total // amount), total * loads[0] // sum(loads)))
    least = 1 if total - largest >= amount - 1 else 0
    given, spare = [largest] + [least] * (amount - 1), total - largest - least * (amount - 1)
    while spare > 0:
        free = [i for i in range(1, amount) if given[i] < largest] or [i for i in range(1, amount) if given[i] < most]
        whole, budget = sum([loads[i] for i in free]), spare
        for i in free:
            addition = min(most - given[i], max(1, budget * loads[i] // whole), spare)
            given[i] = given[i] + addition
            spare = spare - addition
    return np.array(given)


def normal_values(own_key, dims, scale, most, shards=(), kind=jnp.bfloat16):
    drawn = jax.random.normal(own_key, dims, jnp.float32) * scale
    if len(shards) > 0:
        drawn = steps_of(own_key, dims, shards, -0.22, 0.18) * drawn
    return jnp.clip(drawn, min=-most, max=most).astype(kind)


def setup_inputs(seed: int = 0) -> dict:
    splits = jax.random.split(jax.random.key(seed), 15)
    block_input = normal_values(splits[0], (SEQS, LENGTH, D), 1.0, 6.0, ((0, 8), (1, 4)))
    positions = draw_positions(jax.random.fold_in(splits[14], 71), 0)
    norm_gain = jnp.clip(1.0 + 0.1 * jax.random.normal(splits[2], (D,), jnp.float32), 0.5, 1.5).astype(jnp.bfloat16)
    query_weight = normal_values(splits[3], (D, HEADS * HD), D ** -0.5, 0.1875)
    key_weight = normal_values(splits[4], (D, KV_HEADS * HD), D ** -0.5, 0.1875)
    value_weight = normal_values(splits[5], (D, KV_HEADS * HD), D ** -0.5, 0.1875)
    output_weight = normal_values(splits[6], (HEADS * HD, D), (max(1, 4 * HEADS * HD // LENGTH)) ** -0.5, 3.0)
    mixer_gain = jnp.clip(1.0 + 0.1 * jax.random.normal(splits[7], (D,), jnp.float32), 0.5, 1.5).astype(jnp.bfloat16)
    router_weight = normal_values(splits[8], (D, EXPERTS), (4 * D) ** -0.5, 0.09375)
    expert_gate = normal_values(splits[9], (EXPERTS, D, FF), D ** -0.5, 0.1875, ((0, 16),))
    expert_up = normal_values(splits[10], (EXPERTS, D, FF), D ** -0.5, 0.1875, ((0, 16),))
    expert_down = normal_values(splits[11], (EXPERTS, FF, D), (FF // 16) ** -0.5, 1.0, ((0, 16),))
    routes_keys = jax.random.split(jax.random.fold_in(splits[12], 1), SEQS * LENGTH // STRETCH)
    routes_turns = jax.random.permutation(jax.random.fold_in(splits[12], 3), SEQS * LENGTH // STRETCH)
    routes = jax.vmap(lambda own, number: deal_out(jax.random.fold_in(splits[12], 2), own, number, STRETCH, EXPERTS, TOP, CAP, 1))(routes_keys, routes_turns).reshape((SEQS, LENGTH, TOP))
    cotangent = normal_values(splits[13], (SEQS, LENGTH, D), 1.0, 6.0, ((0, 8), (1, 4)))
    return dict(block_input=block_input, positions=positions, norm_gain=norm_gain, query_weight=query_weight, key_weight=key_weight, value_weight=value_weight, output_weight=output_weight, mixer_gain=mixer_gain, router_weight=router_weight, expert_gate=expert_gate, expert_up=expert_up, expert_down=expert_down, routes=routes, cotangent=cotangent)


@jax.custom_vjp
def low(v):
    return lax.optimization_barrier(v.astype(jnp.bfloat16)).astype(jnp.float32)

@jax.custom_vjp
def low_back(v):
    return v

def low_keep(v):
    return (low(v), None)

def low_pass(kept, grad):
    return (grad,)

def back_keep(v):
    return (v, None)

def back_low(kept, grad):
    return (low(grad),)
low.defvjp(low_keep, low_pass)
low_back.defvjp(back_keep, back_low)
EPS = 1e-06
THETA = 10000.0
NEG = -1e+30
HIGH = lax.Precision.HIGHEST

def rms_norm(values, gain):
    return values * lax.rsqrt(lax.optimization_barrier(jnp.mean(values * values, axis=-1, keepdims=True)) + EPS) * gain

def rotate(values, places):
    half = values.shape[-1] // 2
    freqs = THETA ** (-jnp.arange(half, dtype=jnp.float32) * 2.0 / values.shape[-1])
    angle = places.astype(jnp.float32)[:, None] * freqs[None, :]
    cosine = jnp.cos(angle)[:, None, :]
    sine = jnp.sin(angle)[:, None, :]
    first = values[..., :half]
    second = values[..., half:]
    return jnp.concatenate([first * cosine - second * sine, second * cosine + first * sine], axis=-1)

def seq_tables(route):
    blocks = route.reshape(N_CTX, STRETCH * TOP)
    onehot = (blocks[:, :, None] == jnp.arange(EXPERTS, dtype=jnp.int32)[None, None, :]).astype(jnp.int32)
    rank = lax.optimization_barrier(jnp.sum((jnp.cumsum(onehot, axis=1) - 1) * onehot, axis=2))
    block_id = jnp.arange(N_CTX, dtype=jnp.int32)[:, None]
    slot = (blocks * (N_CTX * CAP) + block_id * CAP + rank).reshape(LENGTH * TOP).astype(jnp.int32)
    pair = jnp.full((EXPERTS * N_CTX * CAP,), LENGTH * TOP, jnp.int32).at[slot].set(jnp.arange(LENGTH * TOP, dtype=jnp.int32))
    source = jnp.where(pair < LENGTH * TOP, pair // TOP, LENGTH).astype(jnp.int32)
    return (slot, source)

def layer_seq(weights, inputs, places, route):
    gain_one, w_query, w_key, w_value, w_output, gain_two, w_router, e_gate, e_up, e_down = weights
    groups = HEADS // KV_HEADS
    hidden_one = low(rms_norm(inputs, gain_one))
    query_pre = low_back(jnp.dot(hidden_one, w_query, precision=HIGH)).reshape(LENGTH, HEADS, HD)
    key_pre = low_back(jnp.dot(hidden_one, w_key, precision=HIGH)).reshape(LENGTH, KV_HEADS, HD)
    value = low(low_back(jnp.dot(hidden_one, w_value, precision=HIGH))).reshape(LENGTH, KV_HEADS, HD)
    query = low(rotate(query_pre, places)).reshape(LENGTH, KV_HEADS, groups, HD)
    key = low(rotate(key_pre, places))
    raw = low_back(jnp.einsum('qgrd,kgd->grqk', query, key, precision=HIGH)) * HD ** (-0.5)
    allowed = places[None, :] <= places[:, None]
    scores = jnp.where(allowed[None, None], raw, NEG)
    probs = low(jax.nn.softmax(scores, axis=-1))
    attn = jnp.einsum('grqk,kgd->qgrd', probs, value, precision=HIGH).reshape(LENGTH, HEADS * HD)
    attn = low(low_back(attn))
    mixed = inputs + low_back(jnp.dot(attn, w_output, precision=HIGH))
    hidden_two = low(rms_norm(mixed, gain_two))
    logits = jnp.dot(hidden_two, w_router, precision=HIGH)
    chosen = jnp.take_along_axis(logits, route, axis=1)
    gates = jax.nn.softmax(chosen, axis=-1)
    slot, source = seq_tables(route)
    padded = jnp.concatenate([hidden_two, jnp.zeros((1, D), hidden_two.dtype)], axis=0)
    rows = low_back(padded[source]).reshape(EXPERTS, N_CTX * CAP, D)
    gate_act = low_back(jnp.einsum('erd,edf->erf', rows, e_gate, precision=HIGH))
    up_act = low_back(jnp.einsum('erd,edf->erf', rows, e_up, precision=HIGH))
    product = low(jax.nn.silu(gate_act) * up_act)
    result = low(low_back(jnp.einsum('erf,efd->erd', product, e_down, precision=HIGH))).reshape(EXPERTS * N_CTX * CAP, D)
    picked = result[slot].reshape(LENGTH, TOP, D)
    return mixed + lax.optimization_barrier(jnp.sum(gates[:, :, None] * picked, axis=1))

def reference(block_input, positions, norm_gain, query_weight, key_weight, value_weight, output_weight, mixer_gain, router_weight, expert_gate, expert_up, expert_down, routes, cotangent):
    weights = tuple((w.astype(jnp.float32) for w in (norm_gain, query_weight, key_weight, value_weight, output_weight, mixer_gain, router_weight, expert_gate, expert_up, expert_down)))
    inputs = block_input.astype(jnp.float32)
    step = jax.checkpoint(layer_seq)

    def forward(params, values):
        return lax.map(lambda item: step(params, item[0], item[1], item[2]), (values, positions, routes))
    output, pull = jax.vjp(forward, weights, inputs)
    weight_grads, input_grad = pull(cotangent.astype(jnp.float32))
    return (output.astype(jnp.bfloat16), input_grad.astype(jnp.bfloat16), weight_grads[0], weight_grads[1], weight_grads[2], weight_grads[3], weight_grads[4], weight_grads[5], weight_grads[6], weight_grads[7], weight_grads[8], weight_grads[9])
```

```python
import math

import jax
import jax.numpy as jnp
from jax import lax
from jax.experimental import pallas as pl
from jax.experimental.pallas import tpu as pltpu
from jax.sharding import PartitionSpec as P

HEADS = 16
KV_HEADS = 8
HD = 64


EPS = 1e-06
THETA = 10000.0
NEG = -1e30
HIGH = lax.Precision.HIGHEST
GROUP = ("ctx", "exp")


def rms_norm(values, gain):
    return values * lax.rsqrt(jnp.mean(values * values, axis=-1, keepdims=True) + EPS) * gain


def rotate(values, places):
    half = values.shape[-1] // 2
    freqs = THETA ** (-jnp.arange(half, dtype=jnp.float32) * 2.0 / values.shape[-1])
    angle = places.astype(jnp.float32)[:, None] * freqs[None, :]
    cosine = jnp.cos(angle)[:, None, :]
    sine = jnp.sin(angle)[:, None, :]
    first = values[..., :half]
    second = values[..., half:]
    return jnp.concatenate(
        [first * cosine - second * sine, second * cosine + first * sine], axis=-1
    )


NN = (((1,), (0,)), ((), ()))
NT = (((1,), (1,)), ((), ()))
TN = (((0,), (0,)), ((), ()))


def mul(left, right, dims):
    return lax.dot_general(left, right, dims, preferred_element_type=jnp.float32)


def expert_kernel(
    blocks,
    capacity,
    hidden_ref,
    grads_ref,
    ranks_ref,
    gates_ref,
    gate_ref,
    up_ref,
    down_ref,
    out_ref,
    back_ref,
    dots_ref,
    gate_out,
    up_out,
    down_out,
    gate_acc,
    up_acc,
    down_acc,
):
    f32 = jnp.float32
    bf16 = jnp.bfloat16
    step = pl.program_id(0)
    local = gate_ref.shape[0]
    tokens = hidden_ref.shape[0] // blocks

    @pl.when(step == 0)
    def _():
        gate_acc[...] = jnp.zeros_like(gate_acc)
        up_acc[...] = jnp.zeros_like(up_acc)
        down_acc[...] = jnp.zeros_like(down_acc)

    lanes = lax.broadcasted_iota(jnp.int32, (capacity, tokens), 0).astype(f32)
    for j in range(local):
        picks = []
        shares = []
        rows = []
        grads = []
        for s in range(blocks):
            at = s * local + j
            pick = jnp.where(lanes == ranks_ref[0, at : at + 1, :], 1.0, 0.0)
            shares.append(
                jnp.sum(pick * gates_ref[0, at : at + 1, :], axis=1, keepdims=True)
            )
            picks.append(pick)
            low = pick.astype(bf16)
            span = slice(s * tokens, (s + 1) * tokens)
            rows.append(mul(low, hidden_ref[span, :], NN).astype(bf16))
            grads.append(mul(low, grads_ref[span, :], NN))
        row = jnp.concatenate(rows, axis=0)
        grad = jnp.concatenate(grads, axis=0)
        share = jnp.concatenate(shares, axis=0)
        gate_act = mul(row, gate_ref[j], NN)
        up_act = mul(row, up_ref[j], NN)
        sig = 1.0 / (1.0 + jnp.exp(-gate_act))
        silu = gate_act * sig
        product = (silu * up_act).astype(bf16)
        result = mul(product, down_ref[j], NN).astype(bf16).astype(f32)
        dots = jnp.sum(result * grad, axis=1, keepdims=True)
        result_d = (share * grad).astype(bf16)
        weighed = (share * result).astype(bf16)
        down_acc[j] += mul(product, result_d, TN)
        product_d = mul(result_d, down_ref[j], NT)
        gate_low = (product_d * up_act * (sig * (1.0 + gate_act * (1.0 - sig)))).astype(bf16)
        up_low = (product_d * silu).astype(bf16)
        gate_acc[j] += mul(row, gate_low, TN)
        up_acc[j] += mul(row, up_low, TN)
        row_d = (mul(gate_low, gate_ref[j], NT) + mul(up_low, up_ref[j], NT)).astype(bf16)
        for s in range(blocks):
            at = s * local + j
            part = slice(s * capacity, (s + 1) * capacity)
            span = slice(s * tokens, (s + 1) * tokens)
            dots_ref[0, at : at + 1, :] = jnp.sum(
                picks[s] * dots[part], axis=0, keepdims=True
            )
            low = picks[s].astype(bf16)
            out_piece = mul(low, weighed[part], TN)
            back_piece = mul(low, row_d[part], TN)
            if j > 0:
                out_piece = out_piece + out_ref[span, :].astype(f32)
                back_piece = back_piece + back_ref[span, :].astype(f32)
            out_ref[span, :] = out_piece.astype(bf16)
            back_ref[span, :] = back_piece.astype(bf16)

    @pl.when(step == pl.num_programs(0) - 1)
    def _():
        gate_out[...] = gate_acc[...].astype(bf16)
        up_out[...] = up_acc[...].astype(bf16)
        down_out[...] = down_acc[...].astype(bf16)


def run_experts(hidden, grads, marked, e_gate, e_up, e_down, capacity):
    owners, local, tokens = marked.shape
    width, inner = e_gate.shape[1:]
    blocks = 2
    steps = owners // blocks
    chosen = marked >= 0.0
    upper = (
        jnp.arange(tokens, dtype=jnp.int32)[:, None] <= jnp.arange(tokens, dtype=jnp.int32)[None, :]
    ).astype(jnp.bfloat16)
    counts = jnp.dot(
        chosen.astype(jnp.bfloat16).reshape(owners * local, tokens),
        upper,
        preferred_element_type=jnp.float32,
    ).reshape(owners, local, tokens)
    ranks = jnp.where(chosen, counts - 1.0, -1.0).reshape(steps, blocks * local, tokens)
    gates = jnp.maximum(marked, 0.0).reshape(steps, blocks * local, tokens)
    token_spec = pl.BlockSpec((blocks * tokens, width), lambda i: (i, 0))
    small_spec = pl.BlockSpec((1, blocks * local, tokens), lambda i: (i, 0, 0))
    whole = lambda shape: pl.BlockSpec(
        shape, lambda i: (0, 0, 0), pipeline_mode=pl.Buffered(1)
    )
    wide = (local, width, inner)
    tall = (local, inner, width)
    flops = 2 * owners * local * capacity * width * (9 * inner + 4 * tokens)
    return pl.pallas_call(
        lambda *refs: expert_kernel(blocks, capacity, *refs),
        grid=(steps,),
        in_specs=[
            token_spec,
            token_spec,
            small_spec,
            small_spec,
            whole(wide),
            whole(wide),
            whole(tall),
        ],
        out_specs=[token_spec, token_spec, small_spec, whole(wide), whole(wide), whole(tall)],
        out_shape=[
            jax.ShapeDtypeStruct(hidden.shape, jnp.bfloat16),
            jax.ShapeDtypeStruct(hidden.shape, jnp.bfloat16),
            jax.ShapeDtypeStruct(gates.shape, jnp.float32),
            jax.ShapeDtypeStruct(wide, jnp.bfloat16),
            jax.ShapeDtypeStruct(wide, jnp.bfloat16),
            jax.ShapeDtypeStruct(tall, jnp.bfloat16),
        ],
        scratch_shapes=[
            pltpu.VMEM(wide, jnp.float32),
            pltpu.VMEM(wide, jnp.float32),
            pltpu.VMEM(tall, jnp.float32),
        ],
        compiler_params=pltpu.CompilerParams(
            dimension_semantics=("arbitrary",), vmem_limit_bytes=56 * 1024 * 1024
        ),
        cost_estimate=pl.CostEstimate(
            flops=flops, bytes_accessed=8 * hidden.size + 12 * e_gate.size, transcendentals=0
        ),
    )(hidden, grads, ranks, gates, e_gate, e_up, e_down)


def swap(values):
    return lax.ppermute(values, "dp", [(0, 1), (1, 0)])


def dp_sum(values):
    if lax.axis_size("dp") == 2:
        return values.astype(jnp.float32) + swap(values).astype(jnp.float32)
    return lax.psum(values, "dp").astype(jnp.float32)


def dp_share(values):
    if lax.axis_size("dp") == 2:
        part = values.shape[1] // 2
        me = lax.axis_index("dp")
        other = lax.dynamic_slice_in_dim(values, (1 - me) * part, part, axis=1)
        return (lax.dynamic_slice_in_dim(values, me * part, part, axis=1), swap(other))
    total = lax.psum_scatter(values, "dp", scatter_dimension=1, tiled=True)
    return (total, jnp.zeros_like(total))


def spread(values, axes, count):
    copies = jnp.broadcast_to(values[None], (count,) + values.shape)
    return lax.all_to_all(copies, axes, split_axis=0, concat_axis=0, tiled=True)


def body(
    block_input,
    positions,
    norm_gain,
    query_weight,
    key_weight,
    value_weight,
    output_weight,
    mixer_gain,
    router_weight,
    expert_gate,
    expert_up,
    expert_down,
    routes,
    cotangent,
):
    f32 = jnp.float32
    bf16 = jnp.bfloat16
    rows = block_input.shape[1]
    width = block_input.shape[2]
    groups = HEADS // KV_HEADS
    experts = router_weight.shape[1]
    local_experts = expert_gate.shape[0]
    owners = experts // local_experts
    capacity = rows * routes.shape[2] * 2 // experts
    places = positions[0]
    length = places.shape[0]
    own_places = lax.dynamic_slice_in_dim(places, lax.axis_index("ctx") * rows, rows)
    span = math.gcd(length, 512)
    blocks = length // span
    scale = HD ** (-0.5)
    inputs = block_input[0].astype(f32)
    grad_out = cotangent[0].astype(f32)
    grads_all = lax.all_gather(cotangent[0], GROUP, axis=0, tiled=True)
    gain_one = norm_gain.astype(f32)
    gain_two = mixer_gain.astype(f32)
    hidden_one = rms_norm(inputs, gain_one).astype(bf16)
    query_pre = jnp.dot(hidden_one, query_weight, preferred_element_type=f32).reshape(
        rows, HEADS, HD
    )
    key_pre = jnp.dot(hidden_one, key_weight, preferred_element_type=f32).reshape(
        rows, KV_HEADS, HD
    )
    value_low = jnp.dot(hidden_one, value_weight, preferred_element_type=f32).astype(bf16)
    query_low = rotate(query_pre, own_places).astype(bf16).reshape(rows, KV_HEADS, groups, HD)
    key_low = rotate(key_pre, own_places).astype(bf16).reshape(rows, KV_HEADS * HD)
    ranks = length // rows
    pairs_all = spread(jnp.stack([key_low, value_low]), "ctx", ranks)
    keys_all = pairs_all[:, 0].reshape(length, KV_HEADS * HD)
    values_all = pairs_all[:, 1].reshape(length, KV_HEADS * HD)
    key_blocks = keys_all.reshape(blocks, span, KV_HEADS, HD)
    value_blocks = values_all.reshape(blocks, span, KV_HEADS, HD)
    place_blocks = places.reshape(blocks, span)

    def scores_of(key_block, place_block):
        raw = jnp.einsum("qgrd,kgd->grqk", query_low, key_block, preferred_element_type=f32) * scale
        allowed = place_block[None, :] <= own_places[:, None]
        return (jnp.where(allowed[None, None], raw, NEG), allowed)

    def max_step(carry, item):
        top_score, total = carry
        scores, allowed = scores_of(item[0], item[1])
        new_top = jnp.maximum(top_score, jnp.max(scores, axis=-1))
        terms = jnp.where(allowed[None, None], jnp.exp(scores - new_top[..., None]), 0.0)
        total = total * jnp.exp(top_score - new_top) + jnp.sum(terms, axis=-1)
        return ((new_top, total), None)

    start = (jnp.full((KV_HEADS, groups, rows), NEG, f32), jnp.zeros((KV_HEADS, groups, rows), f32))
    (top_score, total), _ = lax.scan(max_step, start, (key_blocks, place_blocks))
    log_total = top_score + jnp.log(total)

    def value_step(accum, item):
        scores, _ = scores_of(item[0], item[2])
        probs_low = jnp.exp(scores - log_total[..., None]).astype(bf16)
        return (
            accum + jnp.einsum("grqk,kgd->qgrd", probs_low, item[1], preferred_element_type=f32),
            None,
        )

    attn_f32, _ = lax.scan(
        value_step,
        jnp.zeros((rows, KV_HEADS, groups, HD), f32),
        (key_blocks, value_blocks, place_blocks),
    )
    attn_low = attn_f32.reshape(rows, HEADS * HD).astype(bf16)
    mixed = inputs + jnp.dot(attn_low, output_weight, preferred_element_type=f32)
    hidden_two = rms_norm(mixed, gain_two).astype(bf16)
    logits = jnp.dot(hidden_two, router_weight, preferred_element_type=f32)
    route = routes[0]
    onehot = jnp.any(
        route[:, :, None] == jnp.arange(experts, dtype=jnp.int32)[None, None, :], axis=1
    )
    top_logit = jnp.max(jnp.where(onehot, logits, -jnp.inf), axis=1, keepdims=True)
    powers = jnp.where(onehot, jnp.exp(jnp.minimum(logits - top_logit, 0.0)), 0.0)
    gates = powers / jnp.sum(powers, axis=1, keepdims=True)
    marked = lax.all_to_all(
        jnp.where(onehot, gates, -1.0).T.reshape(owners, local_experts, rows),
        GROUP,
        split_axis=0,
        concat_axis=0,
        tiled=True,
    )
    hidden_all = lax.all_gather(hidden_two, GROUP, axis=0, tiled=True)
    out_parts, back_parts, dots, gate_part, up_part, down_part = run_experts(
        hidden_all, grads_all, marked, expert_gate, expert_up, expert_down, capacity
    )
    gate_d = lax.all_to_all(
        dots.reshape(owners, local_experts, rows), GROUP, split_axis=0, concat_axis=0, tiled=True
    )
    gate_d = gate_d.reshape(experts, rows).T
    hidden_two_d = lax.psum_scatter(back_parts, GROUP, scatter_dimension=0, tiled=True).astype(f32)
    gate_share, up_share, down_share = dp_share(gate_part), dp_share(up_part), dp_share(down_part)
    out_parts, hidden_two_d = lax.optimization_barrier((out_parts, hidden_two_d))
    added = lax.psum_scatter(out_parts, GROUP, scatter_dimension=0, tiled=True).astype(f32)
    logits_d = gates * (gate_d - jnp.sum(gates * gate_d, axis=1, keepdims=True))
    hidden_two_d = hidden_two_d + jnp.dot(logits_d, router_weight.astype(f32).T, precision=HIGH)
    router_part = jnp.dot(logits_d.T, hidden_two.astype(f32), precision=HIGH)
    _, norm_two_pull = jax.vjp(rms_norm, mixed, gain_two)
    mixed_part, gain_two_part = norm_two_pull(hidden_two_d)
    mixed_d = grad_out + mixed_part
    mixed_low = mixed_d.astype(bf16)
    output_part = jnp.dot(attn_low.T, mixed_low, preferred_element_type=f32).astype(bf16)
    attn_d = (
        jnp.dot(mixed_low, output_weight.T, preferred_element_type=f32)
        .astype(bf16)
        .reshape(rows, KV_HEADS, groups, HD)
    )
    delta = jnp.transpose(jnp.sum(attn_d.astype(f32) * attn_f32, axis=-1), (1, 2, 0))

    def grad_step(query_d, item):
        key_block, value_block, place_block = item
        scores, _ = scores_of(key_block, place_block)
        probs = jnp.exp(scores - log_total[..., None])
        probs_low = probs.astype(bf16)
        value_piece = jnp.einsum("grqk,qgrd->kgd", probs_low, attn_d, preferred_element_type=f32)
        probs_d = jnp.einsum("qgrd,kgd->grqk", attn_d, value_block, preferred_element_type=f32)
        scores_d = (probs * (probs_d - delta[..., None]) * scale).astype(bf16)
        query_d = query_d + jnp.einsum(
            "grqk,kgd->qgrd", scores_d, key_block, preferred_element_type=f32
        )
        key_piece = jnp.einsum("grqk,qgrd->kgd", scores_d, query_low, preferred_element_type=f32)
        return (
            query_d,
            (key_piece.reshape(span, KV_HEADS * HD), value_piece.reshape(span, KV_HEADS * HD)),
        )

    query_d, (keys_d, values_d) = lax.scan(
        grad_step,
        jnp.zeros((rows, KV_HEADS, groups, HD), f32),
        (key_blocks, value_blocks, place_blocks),
    )
    going = jnp.stack([keys_d.reshape(length, -1), values_d.reshape(length, -1)]).astype(bf16)
    going = going.reshape(2, ranks, rows, KV_HEADS * HD).transpose(1, 0, 2, 3)
    going, gate_share, up_share, down_share = lax.optimization_barrier(
        (going, gate_share, up_share, down_share)
    )
    come = lax.all_to_all(going, "ctx", split_axis=0, concat_axis=0, tiled=True)
    come, output_part = lax.optimization_barrier((come, output_part))
    key_own, value_own = jnp.sum(come.astype(f32), axis=0)
    _, query_pull = jax.vjp(lambda v: rotate(v, own_places), query_pre)
    query_back = (
        query_pull(query_d.reshape(rows, HEADS, HD))[0].reshape(rows, HEADS * HD).astype(bf16)
    )
    _, key_pull = jax.vjp(lambda v: rotate(v, own_places), key_pre)
    key_back = (
        key_pull(key_own.reshape(rows, KV_HEADS, HD))[0].reshape(rows, KV_HEADS * HD).astype(bf16)
    )
    value_back = value_own.astype(bf16)
    back = jnp.concatenate([query_back, key_back, value_back], axis=1)
    late_part = jnp.dot(hidden_one.T, back, preferred_element_type=f32).astype(bf16)
    hidden_one_d = jnp.dot(query_back, query_weight.T, preferred_element_type=f32)
    hidden_one_d = hidden_one_d + jnp.dot(key_back, key_weight.T, preferred_element_type=f32)
    hidden_one_d = hidden_one_d + jnp.dot(value_back, value_weight.T, preferred_element_type=f32)
    _, norm_one_pull = jax.vjp(rms_norm, inputs, gain_one)
    input_part, gain_one_part = norm_one_pull(hidden_one_d)
    input_grad = (mixed_d + input_part).astype(bf16)
    output_part, added = lax.optimization_barrier((output_part, added))
    output = (mixed + added).astype(bf16)
    output_sum = lax.psum_scatter(output_part, GROUP, scatter_dimension=0, tiled=True)
    late_part, output_sum = lax.optimization_barrier((late_part, output_sum))
    late_sum = lax.psum_scatter(late_part, GROUP, scatter_dimension=0, tiled=True)
    output_sum = dp_sum(output_sum).astype(bf16)
    output_total = lax.all_gather(output_sum, GROUP, axis=0, tiled=True).astype(f32)
    late_sum = dp_sum(late_sum).astype(bf16)
    late_total = lax.all_gather(late_sum, GROUP, axis=0, tiled=True).astype(f32)
    few = -(-(experts + 2) // owners)
    small = jnp.concatenate(
        [
            router_part,
            gain_one_part[None],
            gain_two_part[None],
            jnp.zeros((few * owners - experts - 2, width), f32),
        ],
        axis=0,
    ).reshape(owners, few, width)
    small = lax.all_to_all(small, GROUP, split_axis=0, concat_axis=0, tiled=True)
    small = dp_sum(jnp.sum(small, axis=0))
    small = spread(small, GROUP, owners).reshape(few * owners, width)
    wide = query_back.shape[1]
    kv_wide = key_back.shape[1]
    shared = (
        small[experts],
        late_total[:, :wide],
        late_total[:, wide : wide + kv_wide],
        late_total[:, wide + kv_wide :],
        output_total,
        small[experts + 1],
        small[:experts].T,
    )
    owned = tuple(
        own.astype(f32) + other.astype(f32) for own, other in (gate_share, up_share, down_share)
    )
    return (
        output[None],
        input_grad[None],
        shared[0],
        shared[1],
        shared[2],
        shared[3],
        shared[4],
        shared[5],
        shared[6],
        owned[0],
        owned[1],
        owned[2],
    )


def solution(mesh):
    return jax.shard_map(
        body,
        mesh=mesh,
        in_specs=(
            P(("dp", "exp"), "ctx", None),
            P(("dp", "exp"), None),
            P(),
            P(),
            P(),
            P(),
            P(),
            P(),
            P(),
            P(("ctx", "exp"), None, None),
            P(("ctx", "exp"), None, None),
            P(("ctx", "exp"), None, None),
            P(("dp", "exp"), "ctx", None),
            P(("dp", "exp"), "ctx", None),
        ),
        out_specs=(
            P(("dp", "exp"), "ctx", None),
            P(("dp", "exp"), "ctx", None),
            P(),
            P(),
            P(),
            P(),
            P(),
            P(),
            P(),
            P(("ctx", "exp"), "dp", None),
            P(("ctx", "exp"), "dp", None),
            P(("ctx", "exp"), "dp", None),
        ),
        check_vma=False,
    )
```
